32 devices in a mesh: depth: 8 (over y, x, core), filt: 4 (over z).
Axes of the slice: x: 2, y: 2, z: 4, core: 2. Of those that a mesh axis runs over, the one named last changes fastest.
Arguments:
- upper_level: bfloat16 [64, 32, 16, 256], P(None, 'depth', 'filt'), may hold values from -6 to 6
- stride_weight: bfloat16 [8, 128, 64], P(None, 'filt'), may hold values from -0.25 to 0.25
- middle_weight: bfloat16 [27, 128, 128], P(None, 'filt'), may hold values from -0.109375 to 0.109375
- last_weight: bfloat16 [27, 128, 128], P(None, 'filt'), may hold values from -0.109375 to 0.109375
- cotangent: bfloat16 [128, 16, 8, 128], P('filt', 'depth'), may hold values from -0.046875 to 0.046875
Outputs:
- result: bfloat16 [128, 16, 8, 128], P('filt', 'depth')
- grad_stride: float32 [8, 128, 64], P(None, 'filt')
- grad_middle: float32 [27, 128, 128], P(None, 'filt')
- grad_last: float32 [27, 128, 128], P(None, 'filt')
The draws below stay inside these ranges and needn't reach their ends.
All inputs are finite; a program needn't handle non-finite values.
Results may differ from the reference program's by a relative error of at most 0.0059.
Values may be sent and summed in bfloat16 or wider, within the bound.
A program may use at most 64 MiB of HBM per device.

```python
import jax
import jax.numpy as jnp
from jax import lax

C = 128
CIN = 64
W = 128
H = 8
OD = 16


def steps_of(key, extent, shards, smallest, largest):
    factor_of = 1.0
    for position, blocks in shards:
        heights = jax.random.uniform(jax.random.fold_in(jax.random.fold_in(key, 6), position), (blocks,), jnp.float32, smallest / len(shards), largest / len(shards))
        factor_of = factor_of * jnp.repeat(jnp.exp(heights), extent[position] // blocks).reshape((-1,) + (1,) * (len(extent) - 1 - position))
    return factor_of


def normal_values(key, shape, width, reach, cuts=(), held_as=jnp.bfloat16):
    array = jax.random.normal(key, shape, jnp.float32) * width
    if len(cuts) > 0:
        array = steps_of(key, shape, cuts, -0.22, 0.18) * array
    return jnp.clip(array, min=-reach, max=reach).astype(held_as)


def setup_inputs(seed: int = 0) -> dict:
    key_of = jax.random.split(jax.random.key(seed), 6)
    upper_level = normal_values(key_of[0], (CIN, 2 * OD, 2 * H, 2 * W), 1.0, 6.0, ((1, 8), (2, 4)))
    stride_weight = normal_values(key_of[1], (8, C, CIN), (8 * CIN) ** -0.5, 0.25, ((1, 4),))
    middle_weight = normal_values(key_of[2], (27, C, C), (27 * C) ** -0.5, 0.109375, ((1, 4),))
    last_weight = normal_values(key_of[3], (27, C, C), (27 * C) ** -0.5, 0.109375, ((1, 4),))
    cotangent = normal_values(key_of[4], (C, OD, H, W), (OD * H * W) ** -0.5, 0.046875, ((0, 4), (1, 8)))
    return {"upper_level": upper_level, "stride_weight": stride_weight, "middle_weight": middle_weight, "last_weight": last_weight, "cotangent": cotangent}


def stride_conv(upper, weights):
    kernel = weights.reshape(2, 2, 2, weights.shape[1], weights.shape[2])
    return lax.conv_general_dilated(upper[None], kernel, (2, 2, 2), 'VALID', dimension_numbers=('NCDHW', 'DHWOI', 'NCDHW'), precision=lax.Precision.HIGHEST)[0]

def cube_conv(values, weights):
    kernel = weights.reshape(3, 3, 3, weights.shape[1], weights.shape[2])
    return lax.conv_general_dilated(values[None], kernel, (1, 1, 1), [(1, 1), (1, 1), (1, 1)], dimension_numbers=('NCDHW', 'DHWOI', 'NCDHW'), precision=lax.Precision.HIGHEST)[0]

def silu_slope(value):
    sigma = jax.nn.sigmoid(value)
    return sigma * (1.0 + value * (1.0 - sigma))

def reference(upper_level, stride_weight, middle_weight, last_weight, cotangent):
    upper_full = upper_level.astype(jnp.float32)
    stride_full = stride_weight.astype(jnp.float32)
    middle_full = middle_weight.astype(jnp.float32)
    last_full = last_weight.astype(jnp.float32)
    level_pre = stride_conv(upper_full, stride_full)
    level_act = jax.nn.silu(level_pre).astype(jnp.bfloat16)
    level_full = level_act.astype(jnp.float32)
    mid_pre, pull_middle = jax.vjp(cube_conv, level_full, middle_full)
    mid_act = jax.nn.silu(mid_pre).astype(jnp.bfloat16)
    top_pre, pull_last = jax.vjp(cube_conv, mid_act.astype(jnp.float32), last_full)
    result = top_pre.astype(jnp.bfloat16)
    mid_back, grad_last = pull_last(cotangent.astype(jnp.float32))
    mid_delta = (mid_back * silu_slope(mid_pre)).astype(jnp.bfloat16)
    level_back, grad_middle = pull_middle(mid_delta.astype(jnp.float32))
    level_delta = (level_back * silu_slope(level_pre)).astype(jnp.bfloat16)
    _, pull_stride = jax.vjp(lambda kernel: stride_conv(upper_full, kernel), stride_full)
    grad_stride, = pull_stride(level_delta.astype(jnp.float32))
    return (result, grad_stride, grad_middle, grad_last)
```

```python
import functools

import jax
import jax.numpy as jnp
from jax import lax
from jax.experimental import pallas as pl
from jax.experimental.pallas import tpu as pltpu
from jax.sharding import PartitionSpec as P

F32 = jnp.float32
BF16 = jnp.bfloat16
MESH = pl.DeviceIdType.MESH
NEAR = [(z, y) for z in (-1, 0, 1) for y in (-1, 0, 1) if (z, y) != (0, 0)]


def dot(left, right, dims):
    return lax.dot_general(left, right, ((dims[:1], dims[1:]), ((), ())), preferred_element_type=F32)


def silu_slope(value):
    sigma = 1.0 / (1.0 + jnp.exp(-value))
    return sigma * (1.0 + value * (1.0 - sigma))


def silu(value):
    return value / (1.0 + jnp.exp(-value))


def kernel(
    n, m, dl, hl, W,
    up, sw, wm, wl, cot,
    res, gs, gm, gl,
    SW, WM, WL, XL, XM, XG, XD, U, pre_l, pre_m, R,
    pb_s, r1_s, z_s, zr_s, dr_s,
    pb_m, r1_m, z_m, zr_m, dr_m,
    pb_l, r1_l, z_l, zr_l, dr_l,
    near_send, near_recv, swap_send, swap_recv,
    wz_send, wz_recv, wp_send, wp_recv,
    s1_send, s1_recv, s2_send, s2_recv, s3_send, s3_recv, s4_send, s4_recv,
):
    d, f = lax.axis_index("depth"), lax.axis_index("filt")
    oc, C = cot.shape[1], WM.shape[1]
    CI = up.shape[1]
    hb = oc // 2
    half = lax.rem(d, 2)
    mate = d + 1 - 2 * half
    cols = hl * W

    for X in (XL, XM, XG, XD):
        X[...] = jnp.zeros_like(X)

    def at(steps_d, steps_f):
        return (lax.rem(d + steps_d + n, n), lax.rem(f + steps_f + m, m))

    barrier = pltpu.get_barrier_semaphore()
    greet = [(0, k) for k in range(1, m)] + [(y, z) for z, y in NEAR if y != 0]
    greet += [(2 * j, 0) for j in range(1, n // 2)]
    for step in greet:
        pl.semaphore_signal(barrier, inc=1, device_id=at(*step), device_id_type=MESH)
    pl.semaphore_wait(barrier, len(greet))

    def remote(src, dst, send, recv, where):
        return pltpu.make_async_remote_copy(
            src_ref=src, dst_ref=dst, send_sem=send, recv_sem=recv, device_id=where, device_id_type=MESH
        )

    def mul(value, by):
        return pl.multiple_of(value * by, by)

    own = pl.ds(mul(f, oc), oc)
    sends = []
    for k in range(1, m):
        where = at(0, k)
        copy = remote(sw, SW.at[own], swap_send.at[0, k - 1], swap_recv.at[0, k - 1], where)
        copy.start()
        sends.append(copy)

    def weight_out(index, src, dst):
        copies = []
        part = pl.ds(mul(half, hb), hb)
        spot = pl.ds(pl.multiple_of(f * oc + half * hb, hb), hb)
        for k in range(1, m):
            copy = remote(
                src.at[:, part], dst.at[:, spot], wz_send.at[index, k - 1], wz_recv.at[index, k - 1], at(0, k)
            )
            copy.start()
            copies.append(copy)
        return copies

    cot_copies = []
    wm_copies = weight_out(0, wm, WM)
    for k in range(1, m):
        where = at(0, k)
        copy = remote(
            cot.at[:, :, pl.ds(mul(where[1], cols), cols)],
            XG.at[pl.ds(1, dl), own, pl.ds(W, cols)],
            swap_send.at[1, k - 1],
            swap_recv.at[1, k - 1],
            where,
        )
        copy.start()
        cot_copies.append(copy)
    wl_copies = weight_out(1, wl, WL)

    SW[own, :] = sw[...]
    WM[:, own, :] = wm[...]
    WL[:, own, :] = wl[...]
    XG[pl.ds(1, dl), own, pl.ds(W, cols)] = cot[:, :, pl.ds(mul(f, cols), cols)]

    line = lax.broadcasted_iota(jnp.int32, (2 * W, 2 * W), 0)
    column = lax.broadcasted_iota(jnp.int32, (2 * W, 2 * W), 1)
    wanted = jnp.where(column < W, 2 * column, 2 * (column - W) + 1)
    pick = jnp.where(line == wanted, 1.0, 0.0).astype(BF16)
    for plane in range(2 * dl):
        for row in range(2 * hl):
            both = dot(up[plane * 2 * hl + row], pick, (1, 0)).astype(BF16)
            tap = 4 * (plane % 2) + 2 * (row % 2)
            place = ((plane // 2) * hl + row // 2) * W
            U[tap * CI : (tap + 1) * CI, place : place + W] = both[:, :W]
            U[(tap + 1) * CI : (tap + 2) * CI, place : place + W] = both[:, W:]

    lane = lax.rem(lax.broadcasted_iota(jnp.int32, (C, cols), 1), W)

    def before(value):
        return jnp.where(lane == 0, 0.0, pltpu.roll(value, 1, 1))

    def after(value):
        return jnp.where(lane == W - 1, 0.0, pltpu.roll(value, cols - 1, 1))

    def near_copy(index, X, number):
        z, y = NEAR[number]
        src_p, dst_p = {0: ((1, dl), (1, dl)), 1: ((dl, 1), (0, 1)), -1: ((1, 1), (dl + 1, 1))}[y]
        src_c, dst_c = {
            0: ((W, cols), (W, cols)),
            1: ((cols, W), (0, W)),
            -1: ((W, W), (cols + W, W)),
        }[z]
        return remote(
            X.at[pl.ds(*src_p), :, pl.ds(*src_c)],
            X.at[pl.ds(*dst_p), :, pl.ds(*dst_c)],
            near_send.at[index, number],
            near_recv.at[index, number],
            at(y, z),
        )

    def inside(z, y):
        return (f + z >= 0) & (f + z < m) & (d + y >= 0) & (d + y < n)

    def near_start(index, X):
        for number, (z, y) in enumerate(NEAR):
            @pl.when(inside(z, y))
            def _():
                near_copy(index, X, number).start()

    def near_wait(index, X):
        for number, (z, y) in enumerate(NEAR):
            @pl.when(inside(-z, -y))
            def _():
                near_copy(index, X, number).wait_recv()

    def near_end(index, X):
        for number, (z, y) in enumerate(NEAR):
            @pl.when(inside(z, y))
            def _():
                near_copy(index, X, number).wait_send()

    def conv(X, weights, plane):
        total = jnp.zeros((3 * C, cols), F32)
        for a in range(3):
            for b in range(3):
                tap = 9 * a + 3 * b
                left = weights[tap : tap + 3].reshape(3 * C, C)
                total += dot(left, X[plane + a, :, b * W : b * W + cols], (1, 0))
        return before(total[:C]) + total[C : 2 * C] + after(total[2 * C :])

    def conv_back(X, weights, plane):
        parts = []
        for c in range(3):
            total = jnp.zeros((C, cols), F32)
            for a in range(3):
                for b in range(3):
                    right = X[plane + 2 - a, :, (2 - b) * W : (2 - b) * W + cols]
                    total += dot(weights[9 * a + 3 * b + c], right, (0, 0))
            parts.append(total)
        return after(parts[0]) + parts[1] + before(parts[2])

    def weight_grad(D, X, out):
        left = []
        for plane in range(dl):
            value = D[plane + 1, :, W : W + cols]
            wide = value.astype(F32)
            left.append(jnp.concatenate([after(wide).astype(BF16), value, before(wide).astype(BF16)], axis=0))
        for a in range(3):
            for b in range(3):
                total = dot(left[0], X[a, :, b * W : b * W + cols], (1, 1))
                for plane in range(1, dl):
                    total += dot(left[plane], X[plane + a, :, b * W : b * W + cols], (1, 1))
                tap = 9 * a + 3 * b
                out[tap : tap + 3] = total.astype(BF16).reshape(3, m, 2, hb, C)

    def sum_1(index, pb, r1):
        copy = remote(pb.at[:, :, 1 - half], r1, s1_send.at[index], s1_recv.at[index], (mate, f))
        copy.start()
        return [copy]

    def sum_2(index, copies, pb, r1, z, zr):
        copies[0].wait()

        def body(t, carry):
            z[t] = (pb[t, :, half].astype(F32) + r1[t].astype(F32)).astype(BF16)
            return carry

        lax.fori_loop(0, pb.shape[0], body, 0)
        out = []
        for k in range(1, m):
            where = at(0, k)
            copy = remote(
                z.at[:, where[1]], zr.at[k - 1], s2_send.at[index, k - 1], s2_recv.at[index, k - 1], where
            )
            copy.start()
            out.append(copy)
        return out

    def sum_3(index, copies, pb, r1, z, zr, dr):
        for copy in copies:
            copy.wait()
        slot = d // 2

        def body(t, carry):
            total = pb[t, f, half].astype(F32) + r1[t, f].astype(F32)
            for k in range(m - 1):
                total += zr[k, t].astype(F32)
            dr[slot, t] = total.astype(BF16)
            return carry

        lax.fori_loop(0, pb.shape[0], body, 0)
        out = []
        for j in range(1, n // 2):
            copy = remote(
                dr.at[slot], dr.at[slot], s3_send.at[index, j - 1], s3_recv.at[index, j - 1], at(2 * j, 0)
            )
            copy.start()
            out.append(copy)
        return out

    def sum_4(index, copies, dr, out):
        for copy in copies:
            copy.wait()
        part = pl.ds(mul(half, hb), hb)

        def body(t, carry):
            total = dr[0, t].astype(F32)
            for j in range(1, n // 2):
                total += dr[j, t].astype(F32)
            out[t, part, :] = total
            return carry

        lax.fori_loop(0, out.shape[0], body, 0)
        copy = remote(out.at[:, part], out.at[:, part], s4_send.at[index], s4_recv.at[index], (mate, f))
        copy.start()
        return [copy]

    def weight_pass(index, copies, dst):
        out = []
        for k in range(1, m):
            copies[k - 1].wait()
            spot = pl.ds(pl.multiple_of(lax.rem(f - k + m, m) * oc + half * hb, hb), hb)
            copy = remote(
                dst.at[:, spot], dst.at[:, spot], wp_send.at[index, k - 1], wp_recv.at[index, k - 1], (mate, f)
            )
            copy.start()
            out.append(copy)
        return out

    def flat(X, plane):
        return X[plane + 1, :, W : W + cols]

    for copy in sends:
        copy.wait()
    for plane in range(dl):
        value = dot(SW[...], U[:, plane * cols : (plane + 1) * cols], (1, 0))
        pre_l[plane] = value
        XL[plane + 1, :, W : W + cols] = silu(value).astype(BF16)
    near_start(0, XL)
    wm_pass = weight_pass(0, wm_copies, WM)
    for copy in cot_copies:
        copy.wait()
    near_start(1, XG)
    near_wait(0, XL)
    for copy in wm_pass:
        copy.wait()
    for plane in range(dl):
        value = conv(XL, WM, plane)
        pre_m[plane] = value
        XM[plane + 1, :, W : W + cols] = silu(value).astype(BF16)
    near_start(2, XM)
    wl_pass = weight_pass(1, wl_copies, WL)
    near_wait(1, XG)
    for copy in wl_pass:
        copy.wait()

    for plane in range(dl):
        value = conv_back(XG, WL, plane) * silu_slope(pre_m[plane])
        XD[plane + 1, :, W : W + cols] = value.astype(BF16)
    near_start(3, XD)
    weight_grad(XD, XL, pb_m)
    sum_m = sum_1(0, pb_m, r1_m)
    near_wait(2, XM)
    weight_grad(XG, XM, pb_l)
    sum_l = sum_1(1, pb_l, r1_l)
    sum_m = sum_2(0, sum_m, pb_m, r1_m, z_m, zr_m)
    near_wait(3, XD)
    left = []
    for plane in range(dl):
        value = conv_back(XD, WM, plane) * silu_slope(pre_l[plane])
        left.append(value.astype(BF16))
    total = dot(left[0], U[:, :cols], (1, 1))
    for plane in range(1, dl):
        total += dot(left[plane], U[:, plane * cols : (plane + 1) * cols], (1, 1))
    pb_s[...] = total.astype(BF16).reshape(pb_s.shape)
    sum_s = sum_1(2, pb_s, r1_s)
    sum_l = sum_2(1, sum_l, pb_l, r1_l, z_l, zr_l)
    sum_s = sum_2(2, sum_s, pb_s, r1_s, z_s, zr_s)

    for plane in range(dl):
        R[plane] = conv(XM, WL, plane).astype(BF16)
    out_spot = pl.ds(mul(f, cols), cols)
    out_copies = []
    for k in range(1, m):
        where = at(0, k)
        copy = remote(
            R.at[:, pl.ds(mul(where[1], oc), oc)],
            res.at[:, :, out_spot],
            swap_send.at[2, k - 1],
            swap_recv.at[2, k - 1],
            where,
        )
        copy.start()
        out_copies.append(copy)
    res[:, :, out_spot] = R[:, own]

    sum_m = sum_3(0, sum_m, pb_m, r1_m, z_m, zr_m, dr_m)
    sum_l = sum_3(1, sum_l, pb_l, r1_l, z_l, zr_l, dr_l)
    sum_s = sum_3(2, sum_s, pb_s, r1_s, z_s, zr_s, dr_s)
    sum_m = sum_4(0, sum_m, dr_m, gm)
    sum_l = sum_4(1, sum_l, dr_l, gl)
    sum_s = sum_4(2, sum_s, dr_s, gs)
    for copy in out_copies + sum_m + sum_l + sum_s:
        copy.wait()
    for index, X in enumerate((XL, XG, XM, XD)):
        near_end(index, X)


def per_device(n, m, upper_level, stride_weight, middle_weight, last_weight, cotangent):
    oc, dl, H, W = cotangent.shape
    hl = H // m
    C, CI = oc * m, upper_level.shape[0]
    T = middle_weight.shape[0]
    hb = oc // 2
    up = upper_level.transpose(1, 2, 0, 3).reshape(4 * dl * hl, CI, 2 * W)
    sw = stride_weight.transpose(1, 0, 2).reshape(oc, 8 * CI)
    cot = cotangent.transpose(1, 0, 2, 3).reshape(dl, oc, H * W)
    wide = pltpu.VMEM((dl + 2, C, (hl + 2) * W), BF16)

    def sums(count, lanes):
        return [
            pltpu.VMEM((count, m, 2, hb, lanes), BF16),
            pltpu.VMEM((count, m, hb, lanes), BF16),
            pltpu.VMEM((count, m, hb, lanes), BF16),
            pltpu.VMEM((m - 1, count, hb, lanes), BF16),
            pltpu.VMEM((n // 2, count, hb, lanes), BF16),
        ]

    def sems(*shape):
        return [pltpu.SemaphoreType.DMA(shape)] * 2

    res, gs, gm, gl = pl.pallas_call(
        functools.partial(kernel, n, m, dl, hl, W),
        out_shape=(
            jax.ShapeDtypeStruct((dl, oc, H * W), BF16),
            jax.ShapeDtypeStruct((1, oc, 8 * CI), F32),
            jax.ShapeDtypeStruct((T, oc, C), F32),
            jax.ShapeDtypeStruct((T, oc, C), F32),
        ),
        in_specs=[pl.BlockSpec(memory_space=pltpu.VMEM)] * 5,
        out_specs=[pl.BlockSpec(memory_space=pltpu.VMEM)] * 4,
        scratch_shapes=[
            pltpu.VMEM((C, 8 * CI), BF16),
            pltpu.VMEM((T, C, C), BF16),
            pltpu.VMEM((T, C, C), BF16),
            wide, wide, wide, wide,
            pltpu.VMEM((8 * CI, dl * hl * W), BF16),
            pltpu.VMEM((dl, C, hl * W), F32),
            pltpu.VMEM((dl, C, hl * W), F32),
            pltpu.VMEM((dl, C, hl * W), BF16),
            *sums(1, 8 * CI),
            *sums(T, C),
            *sums(T, C),
            *sems(4, 8),
            *sems(3, m - 1),
            *sems(2, m - 1),
            *sems(2, m - 1),
            *sems(3),
            *sems(3, m - 1),
            *sems(3, n // 2 - 1),
            *sems(3),
        ],
        compiler_params=pltpu.CompilerParams(
            collective_id=0, has_side_effects=True, vmem_limit_bytes=52 * 1024 * 1024
        ),
    )(up, sw, middle_weight, last_weight, cot)
    result = res.reshape(dl, oc, H, W).transpose(1, 0, 2, 3)
    grad_stride = gs.reshape(oc, 8, CI).transpose(1, 0, 2)
    return (result, grad_stride, gm, gl)


def solution(mesh):
    weights = P(None, "filt", None)
    cells = P("filt", "depth", None, None)
    return jax.shard_map(
        functools.partial(per_device, mesh.shape["depth"], mesh.shape["filt"]),
        mesh=mesh,
        in_specs=(P(None, "depth", "filt", None), weights, weights, weights, cells),
        out_specs=(cells, weights, weights, weights),
        check_vma=False,
    )
```

```python
import functools

import jax
import jax.numpy as jnp
from jax import lax
from jax.experimental import pallas as pl
from jax.experimental.pallas import tpu as pltpu
from jax.sharding import PartitionSpec as P

F32 = jnp.float32
BF16 = jnp.bfloat16
MESH = pl.DeviceIdType.MESH
NEAR = [(z, y) for z in (-1, 0, 1) for y in (-1, 0, 1) if (z, y) != (0, 0)]


def dot(left, right, dims):
    return lax.dot_general(left, right, ((dims[:1], dims[1:]), ((), ())), preferred_element_type=F32)


def silu_slope(value):
    sigma = 1.0 / (1.0 + jnp.exp(-value))
    return sigma * (1.0 + value * (1.0 - sigma))


def silu(value):
    return value / (1.0 + jnp.exp(-value))


def kernel(
    n, m, dl, hl, W,
    up, sw, wm, wl, cot,
    res, gs, gm, gl,
    SW, WM, WL, XL, XM, XG, XD, U, pre_l, pre_m, R,
    pb_s, r1_s, z_s, pr_s, y_s, zr_s,
    pb_m, r1_m, z_m, pr_m, y_m, zr_m,
    pb_l, r1_l, z_l, pr_l, y_l, zr_l,
    near_send, near_recv, swap_send, swap_recv,
    wz_send, wz_recv, wg_send, wg_recv, wp_send, wp_recv,
    s1_send, s1_recv, s2_send, s2_recv, s3_send, s3_recv, s4_send, s4_recv, s5_send, s5_recv,
):
    d, f = lax.axis_index("depth"), lax.axis_index("filt")
    oc, C = cot.shape[1], WM.shape[1]
    CI = up.shape[1]
    hb = oc // 2
    T = wm.shape[0]
    groups = n // 2
    half, slot = lax.rem(d, 2), d // 2
    mate = d + 1 - 2 * half
    cols = hl * W

    for X in (XL, XM, XG, XD):
        X[...] = jnp.zeros_like(X)
    for X, used in ((WM, T), (WL, T), (pb_m, T), (pb_l, T), (pb_s, 4)):
        if X.shape[0] > used:
            X[used:] = jnp.zeros((X.shape[0] - used,) + X.shape[1:], X.dtype)
    own = pl.ds(pl.multiple_of(f * oc, oc), oc)
    WM[:T, own, :] = wm[...]
    WL[:T, own, :] = wl[...]

    def at(steps_d, steps_f):
        return (lax.rem(d + steps_d + n, n), lax.rem(f + steps_f + m, m))

    barrier = pltpu.get_barrier_semaphore()
    greet = [(0, k) for k in range(1, m)] + [(y, z) for z, y in NEAR if y != 0]
    greet += [(2 * j, 0) for j in range(1, n // 2)]
    for step in greet:
        pl.semaphore_signal(barrier, inc=1, device_id=at(*step), device_id_type=MESH)
    pl.semaphore_wait(barrier, len(greet))

    def remote(src, dst, send, recv, where):
        return pltpu.make_async_remote_copy(
            src_ref=src, dst_ref=dst, send_sem=send, recv_sem=recv, device_id=where, device_id_type=MESH
        )

    def mul(value, by):
        return pl.multiple_of(value * by, by)

    sends = []
    for k in range(1, m):
        where = at(0, k)
        copy = remote(sw, SW.at[own], swap_send.at[0, k - 1], swap_recv.at[0, k - 1], where)
        copy.start()
        sends.append(copy)

    def band(k):
        return pl.ds(pl.multiple_of(lax.rem(f - k + m, m) * oc + half * hb, hb), hb)

    def weight_out(index, dst):
        copies = []
        share = dst.shape[0] // groups
        piece = dst.at[pl.ds(slot * share, share), band(0)]
        for k in range(1, m):
            copy = remote(piece, piece, wz_send.at[index, k - 1], wz_recv.at[index, k - 1], at(0, k))
            copy.start()
            copies.append(copy)
        return copies

    cot_copies = []
    wm_copies = weight_out(0, WM)
    for k in range(1, m):
        where = at(0, k)
        copy = remote(
            cot.at[:, :, pl.ds(mul(where[1], cols), cols)],
            XG.at[pl.ds(1, dl), own, pl.ds(W, cols)],
            swap_send.at[1, k - 1],
            swap_recv.at[1, k - 1],
            where,
        )
        copy.start()
        cot_copies.append(copy)
    wl_copies = weight_out(1, WL)

    SW[own, :] = sw[...]
    XG[pl.ds(1, dl), own, pl.ds(W, cols)] = cot[:, :, pl.ds(mul(f, cols), cols)]

    line = lax.broadcasted_iota(jnp.int32, (2 * W, 2 * W), 0)
    column = lax.broadcasted_iota(jnp.int32, (2 * W, 2 * W), 1)
    wanted = jnp.where(column < W, 2 * column, 2 * (column - W) + 1)
    pick = jnp.where(line == wanted, 1.0, 0.0).astype(BF16)
    for plane in range(2 * dl):
        for row in range(2 * hl):
            both = dot(up[plane * 2 * hl + row], pick, (1, 0)).astype(BF16)
            tap = 4 * (plane % 2) + 2 * (row % 2)
            place = ((plane // 2) * hl + row // 2) * W
            U[tap * CI : (tap + 1) * CI, place : place + W] = both[:, :W]
            U[(tap + 1) * CI : (tap + 2) * CI, place : place + W] = both[:, W:]

    lane = lax.rem(lax.broadcasted_iota(jnp.int32, (C, cols), 1), W)

    def before(value):
        return jnp.where(lane == 0, 0.0, pltpu.roll(value, 1, 1))

    def after(value):
        return jnp.where(lane == W - 1, 0.0, pltpu.roll(value, cols - 1, 1))

    def near_copy(index, X, number):
        z, y = NEAR[number]
        src_p, dst_p = {0: ((1, dl), (1, dl)), 1: ((dl, 1), (0, 1)), -1: ((1, 1), (dl + 1, 1))}[y]
        src_c, dst_c = {
            0: ((W, cols), (W, cols)),
            1: ((cols, W), (0, W)),
            -1: ((W, W), (cols + W, W)),
        }[z]
        return remote(
            X.at[pl.ds(*src_p), :, pl.ds(*src_c)],
            X.at[pl.ds(*dst_p), :, pl.ds(*dst_c)],
            near_send.at[index, number],
            near_recv.at[index, number],
            at(y, z),
        )

    def inside(z, y):
        return (f + z >= 0) & (f + z < m) & (d + y >= 0) & (d + y < n)

    def near_start(index, X):
        for number, (z, y) in enumerate(NEAR):
            @pl.when(inside(z, y))
            def _():
                near_copy(index, X, number).start()

    def near_wait(index, X):
        for number, (z, y) in enumerate(NEAR):
            @pl.when(inside(-z, -y))
            def _():
                near_copy(index, X, number).wait_recv()

    def near_end(index, X):
        for number, (z, y) in enumerate(NEAR):
            @pl.when(inside(z, y))
            def _():
                near_copy(index, X, number).wait_send()

    def conv(X, weights, plane):
        total = jnp.zeros((3 * C, cols), F32)
        for a in range(3):
            for b in range(3):
                tap = 9 * a + 3 * b
                left = weights[tap : tap + 3].reshape(3 * C, C)
                total += dot(left, X[plane + a, :, b * W : b * W + cols], (1, 0))
        return before(total[:C]) + total[C : 2 * C] + after(total[2 * C :])

    def conv_back(X, weights, plane):
        parts = []
        for c in range(3):
            total = jnp.zeros((C, cols), F32)
            for a in range(3):
                for b in range(3):
                    right = X[plane + 2 - a, :, (2 - b) * W : (2 - b) * W + cols]
                    total += dot(weights[9 * a + 3 * b + c], right, (0, 0))
            parts.append(total)
        return after(parts[0]) + parts[1] + before(parts[2])

    def weight_grad(D, X, out):
        left = []
        for plane in range(dl):
            value = D[plane + 1, :, W : W + cols]
            wide = value.astype(F32)
            left.append(jnp.concatenate([after(wide).astype(BF16), value, before(wide).astype(BF16)], axis=0))
        for a in range(3):
            for b in range(3):
                total = dot(left[0], X[a, :, b * W : b * W + cols], (1, 1))
                for plane in range(1, dl):
                    total += dot(left[plane], X[plane + a, :, b * W : b * W + cols], (1, 1))
                tap = 9 * a + 3 * b
                out[tap : tap + 3] = total.astype(BF16).reshape(3, m, 2, hb, C)

    def sum_1(index, pb, r1):
        copy = remote(pb.at[:, :, 1 - half], r1, s1_send.at[index], s1_recv.at[index], (mate, f))
        copy.start()
        return [copy]

    def sum_2(index, copies, pb, r1, z, pr):
        copies[0].wait()

        def body(t, carry):
            z[t] = (pb[t, :, half].astype(F32) + r1[t].astype(F32)).astype(BF16)
            return carry

        lax.fori_loop(0, pb.shape[0], body, 0)
        share = pb.shape[0] // groups
        out = []
        for j in range(1, groups):
            where = at(2 * j, 0)
            copy = remote(
                z.at[pl.ds((where[0] // 2) * share, share)],
                pr.at[j - 1],
                s2_send.at[index, j - 1],
                s2_recv.at[index, j - 1],
                where,
            )
            copy.start()
            out.append(copy)
        return out

    def sum_3(index, copies, z, pr, y, zr):
        for copy in copies:
            copy.wait()
        share = y.shape[0]

        def body(t, carry):
            total = z[slot * share + t].astype(F32)
            for j in range(groups - 1):
                total += pr[j, t].astype(F32)
            y[t] = total.astype(BF16)
            return carry

        lax.fori_loop(0, share, body, 0)
        out = []
        for k in range(1, m):
            where = at(0, k)
            copy = remote(
                y.at[:, where[1]], zr.at[k - 1], s3_send.at[index, k - 1], s3_recv.at[index, k - 1], where
            )
            copy.start()
            out.append(copy)
        return out

    def sum_4(index, copies, y, zr, out):
        for copy in copies:
            copy.wait()
        share = y.shape[0]
        part = pl.ds(mul(half, hb), hb)

        def body(t, carry):
            total = y[t, f].astype(F32)
            for k in range(m - 1):
                total += zr[k, t].astype(F32)
            out[slot * share + t, part, :] = total
            return carry

        lax.fori_loop(0, share, body, 0)
        piece = out.at[pl.ds(slot * share, share), part]
        copies = []
        for j in range(1, groups):
            copy = remote(piece, piece, s4_send.at[index, j - 1], s4_recv.at[index, j - 1], at(2 * j, 0))
            copy.start()
            copies.append(copy)
        return copies

    def sum_5(index, copies, out):
        for copy in copies:
            copy.wait()
        part = pl.ds(mul(half, hb), hb)
        copy = remote(out.at[:, part], out.at[:, part], s5_send.at[index], s5_recv.at[index], (mate, f))
        copy.start()
        return [copy]

    def weight_spread(index, copies, dst):
        share = dst.shape[0] // groups
        out = []
        for k in range(1, m):
            copies[k - 1].wait()
            piece = dst.at[pl.ds(slot * share, share), band(k)]
            for j in range(1, groups):
                copy = remote(
                    piece, piece, wg_send.at[index, k - 1, j - 1], wg_recv.at[index, k - 1, j - 1], at(2 * j, 0)
                )
                copy.start()
                out.append(copy)
        return out

    def weight_pass(index, copies, dst):
        out = []
        for k in range(1, m):
            for copy in copies[(k - 1) * (groups - 1) : k * (groups - 1)]:
                copy.wait()
            piece = dst.at[:, band(k)]
            copy = remote(piece, piece, wp_send.at[index, k - 1], wp_recv.at[index, k - 1], (mate, f))
            copy.start()
            out.append(copy)
        return out

    for copy in sends:
        copy.wait()
    for plane in range(dl):
        value = dot(SW[...], U[:, plane * cols : (plane + 1) * cols], (1, 0))
        pre_l[plane] = value
        XL[plane + 1, :, W : W + cols] = silu(value).astype(BF16)
    near_start(0, XL)
    wm_pass = weight_spread(0, wm_copies, WM)
    for copy in cot_copies:
        copy.wait()
    near_start(1, XG)
    wm_pass = weight_pass(0, wm_pass, WM)
    wl_pass = weight_spread(1, wl_copies, WL)
    near_wait(0, XL)
    for copy in wm_pass:
        copy.wait()
    for plane in range(dl):
        value = conv(XL, WM, plane)
        pre_m[plane] = value
        XM[plane + 1, :, W : W + cols] = silu(value).astype(BF16)
    near_start(2, XM)
    wl_pass = weight_pass(1, wl_pass, WL)
    near_wait(1, XG)
    for copy in wl_pass:
        copy.wait()

    for plane in range(dl):
        value = conv_back(XG, WL, plane) * silu_slope(pre_m[plane])
        XD[plane + 1, :, W : W + cols] = value.astype(BF16)
    near_start(3, XD)
    near_wait(2, XM)
    weight_grad(XG, XM, pb_l)
    sum_l = sum_1(1, pb_l, r1_l)
    weight_grad(XD, XL, pb_m)
    sum_m = sum_1(0, pb_m, r1_m)
    sum_l = sum_2(1, sum_l, pb_l, r1_l, z_l, pr_l)
    near_wait(3, XD)
    left = []
    for plane in range(dl):
        value = conv_back(XD, WM, plane) * silu_slope(pre_l[plane])
        left.append(value.astype(BF16))
    total = dot(left[0], U[:, :cols], (1, 1))
    for plane in range(1, dl):
        total += dot(left[plane], U[:, plane * cols : (plane + 1) * cols], (1, 1))
    total = total.astype(BF16)
    for pair in range(4):
        pb_s[pair] = total[:, pair * 2 * CI : (pair + 1) * 2 * CI].reshape(pb_s.shape[1:])
    sum_s = sum_1(2, pb_s, r1_s)
    sum_m = sum_2(0, sum_m, pb_m, r1_m, z_m, pr_m)
    sum_s = sum_2(2, sum_s, pb_s, r1_s, z_s, pr_s)
    sum_l = sum_3(1, sum_l, z_l, pr_l, y_l, zr_l)

    for plane in range(dl):
        R[plane] = conv(XM, WL, plane).astype(BF16)
    out_spot = pl.ds(mul(f, cols), cols)
    out_copies = []
    for k in range(1, m):
        where = at(0, k)
        copy = remote(
            R.at[:, pl.ds(mul(where[1], oc), oc)],
            res.at[:, :, out_spot],
            swap_send.at[2, k - 1],
            swap_recv.at[2, k - 1],
            where,
        )
        copy.start()
        out_copies.append(copy)
    res[:, :, out_spot] = R[:, own]

    sum_m = sum_3(0, sum_m, z_m, pr_m, y_m, zr_m)
    sum_s = sum_3(2, sum_s, z_s, pr_s, y_s, zr_s)
    sum_l = sum_4(1, sum_l, y_l, zr_l, gl)
    sum_m = sum_4(0, sum_m, y_m, zr_m, gm)
    sum_s = sum_4(2, sum_s, y_s, zr_s, gs)
    sum_l = sum_5(1, sum_l, gl)
    sum_m = sum_5(0, sum_m, gm)
    sum_s = sum_5(2, sum_s, gs)
    for copy in out_copies + sum_m + sum_l + sum_s:
        copy.wait()
    for index, X in enumerate((XL, XG, XM, XD)):
        near_end(index, X)


def per_device(n, m, upper_level, stride_weight, middle_weight, last_weight, cotangent):
    oc, dl, H, W = cotangent.shape
    hl = H // m
    C, CI = oc * m, upper_level.shape[0]
    T = middle_weight.shape[0]
    hb = oc // 2
    up = upper_level.transpose(1, 2, 0, 3).reshape(4 * dl * hl, CI, 2 * W)
    sw = stride_weight.transpose(1, 0, 2).reshape(oc, 8 * CI)
    cot = cotangent.transpose(1, 0, 2, 3).reshape(dl, oc, H * W)
    wide = pltpu.VMEM((dl + 2, C, (hl + 2) * W), BF16)

    groups = n // 2
    TP, SP = -(-T // groups) * groups, -(-4 // groups) * groups

    def sums(count, lanes):
        share = count // groups
        return [
            pltpu.VMEM((count, m, 2, hb, lanes), BF16),
            pltpu.VMEM((count, m, hb, lanes), BF16),
            pltpu.VMEM((count, m, hb, lanes), BF16),
            pltpu.VMEM((groups - 1, share, m, hb, lanes), BF16),
            pltpu.VMEM((share, m, hb, lanes), BF16),
            pltpu.VMEM((m - 1, share, hb, lanes), BF16),
        ]

    def sems(*shape):
        return [pltpu.SemaphoreType.DMA(shape)] * 2

    res, gs, gm, gl = pl.pallas_call(
        functools.partial(kernel, n, m, dl, hl, W),
        out_shape=(
            jax.ShapeDtypeStruct((dl, oc, H * W), BF16),
            jax.ShapeDtypeStruct((SP, oc, 2 * CI), F32),
            jax.ShapeDtypeStruct((TP, oc, C), F32),
            jax.ShapeDtypeStruct((TP, oc, C), F32),
        ),
        in_specs=[pl.BlockSpec(memory_space=pltpu.VMEM)] * 5,
        out_specs=[pl.BlockSpec(memory_space=pltpu.VMEM)] * 4,
        scratch_shapes=[
            pltpu.VMEM((C, 8 * CI), BF16),
            pltpu.VMEM((TP, C, C), BF16),
            pltpu.VMEM((TP, C, C), BF16),
            wide, wide, wide, wide,
            pltpu.VMEM((8 * CI, dl * hl * W), BF16),
            pltpu.VMEM((dl, C, hl * W), F32),
            pltpu.VMEM((dl, C, hl * W), F32),
            pltpu.VMEM((dl, C, hl * W), BF16),
            *sums(SP, 2 * CI),
            *sums(TP, C),
            *sums(TP, C),
            *sems(4, 8),
            *sems(3, m - 1),
            *sems(2, m - 1),
            *sems(2, m - 1, groups - 1),
            *sems(2, m - 1),
            *sems(3),
            *sems(3, groups - 1),
            *sems(3, m - 1),
            *sems(3, groups - 1),
            *sems(3),
        ],
        compiler_params=pltpu.CompilerParams(
            collective_id=0, has_side_effects=True, vmem_limit_bytes=52 * 1024 * 1024
        ),
    )(up, sw, middle_weight, last_weight, cot)
    result = res.reshape(dl, oc, H, W).transpose(1, 0, 2, 3)
    grad_stride = gs[:4].reshape(4, oc, 2, CI).transpose(0, 2, 1, 3).reshape(8, oc, CI)
    return (result, grad_stride, gm[:T], gl[:T])


def solution(mesh):
    weights = P(None, "filt", None)
    cells = P("filt", "depth", None, None)
    return jax.shard_map(
        functools.partial(per_device, mesh.shape["depth"], mesh.shape["filt"]),
        mesh=mesh,
        in_specs=(P(None, "depth", "filt", None), weights, weights, weights, cells),
        out_specs=(cells, weights, weights, weights),
        check_vma=False,
    )
```

```python
import functools

import jax
import jax.numpy as jnp
from jax import lax
from jax.experimental import pallas as pl
from jax.experimental.pallas import tpu as pltpu
from jax.sharding import PartitionSpec as P

F32 = jnp.float32
BF16 = jnp.bfloat16
MESH = pl.DeviceIdType.MESH
CHUNKS = (15, 12, 15, 12, 4)
NEAR = [(z, y) for z in (-1, 0, 1) for y in (-1, 0, 1) if (z, y) != (0, 0)]


def dot(left, right, dims):
    return lax.dot_general(left, right, ((dims[:1], dims[1:]), ((), ())), preferred_element_type=F32)


def silu_slope(value):
    sigma = 1.0 / (1.0 + jnp.exp(-value))
    return sigma * (1.0 + value * (1.0 - sigma))


def silu(value):
    return value / (1.0 + jnp.exp(-value))


def kernel(
    n, m, dl, hl, W,
    up, sw, wm, wl, cot,
    *refs,
):
    res, *outs = refs[:6]
    SW, WM, WL, XL, XM, XG, XD, U, pre_l, pre_m, R = refs[6:17]
    bufs = [refs[17 + 6 * i : 23 + 6 * i] for i in range(5)]
    (
    near_send, near_recv, swap_send, swap_recv,
    wz_send, wz_recv, wg_send, wg_recv, wp_send, wp_recv,
    s1_send, s1_recv, s2_send, s2_recv, s3_send, s3_recv, s4_send, s4_recv, s5_send, s5_recv,
    ) = refs[47:]
    d, f = lax.axis_index("depth"), lax.axis_index("filt")
    oc, C = cot.shape[1], WM.shape[1]
    CI = up.shape[1]
    hb = oc // 2
    T = wm.shape[0]
    groups = n // 2
    half, slot = lax.rem(d, 2), d // 2
    mate = d + 1 - 2 * half
    cols = hl * W

    for X in (XL, XM, XG, XD):
        X[...] = jnp.zeros_like(X)
    for X, used in ((WM, T), (WL, T), *((bufs[i][0], CHUNKS[i]) for i in range(5))):
        if X.shape[0] > used:
            X[used:] = jnp.zeros((X.shape[0] - used,) + X.shape[1:], X.dtype)
    own = pl.ds(pl.multiple_of(f * oc, oc), oc)
    WM[:T, own, :] = wm[...]
    WL[:T, own, :] = wl[...]
    for tap in range(8):
        SW[own, tap * CI : (tap + 1) * CI] = sw[tap]

    def at(steps_d, steps_f):
        return (lax.rem(d + steps_d + n, n), lax.rem(f + steps_f + m, m))

    barrier = pltpu.get_barrier_semaphore()
    greet = [(0, k) for k in range(1, m)] + [(y, z) for z, y in NEAR if y != 0]
    greet += [(2 * j, 0) for j in range(1, n // 2)]
    for step in greet:
        pl.semaphore_signal(barrier, inc=1, device_id=at(*step), device_id_type=MESH)
    pl.semaphore_wait(barrier, len(greet))

    def remote(src, dst, send, recv, where):
        return pltpu.make_async_remote_copy(
            src_ref=src, dst_ref=dst, send_sem=send, recv_sem=recv, device_id=where, device_id_type=MESH
        )

    def mul(value, by):
        return pl.multiple_of(value * by, by)

    sends = []
    for k in range(1, m):
        where = at(0, k)
        copy = remote(SW.at[own], SW.at[own], swap_send.at[0, k - 1], swap_recv.at[0, k - 1], where)
        copy.start()
        sends.append(copy)

    def band(k):
        return pl.ds(pl.multiple_of(lax.rem(f - k + m, m) * oc + half * hb, hb), hb)

    def weight_out(index, dst):
        copies = []
        share = dst.shape[0] // groups
        piece = dst.at[pl.ds(slot * share, share), band(0)]
        for k in range(1, m):
            copy = remote(piece, piece, wz_send.at[index, k - 1], wz_recv.at[index, k - 1], at(0, k))
            copy.start()
            copies.append(copy)
        return copies

    wm_copies = weight_out(0, WM)
    XG[pl.ds(1, dl), own, pl.ds(W, cols)] = cot[:, :, pl.ds(mul(f, cols), cols)]

    line = lax.broadcasted_iota(jnp.int32, (2 * W, 2 * W), 0)
    column = lax.broadcasted_iota(jnp.int32, (2 * W, 2 * W), 1)
    wanted = jnp.where(column < W, 2 * column, 2 * (column - W) + 1)
    pick = jnp.where(line == wanted, 1.0, 0.0).astype(BF16)
    for plane in range(2 * dl):
        for row in range(2 * hl):
            both = dot(up[plane * 2 * hl + row], pick, (1, 0)).astype(BF16)
            tap = 4 * (plane % 2) + 2 * (row % 2)
            place = ((plane // 2) * hl + row // 2) * W
            U[tap * CI : (tap + 1) * CI, place : place + W] = both[:, :W]
            U[(tap + 1) * CI : (tap + 2) * CI, place : place + W] = both[:, W:]

    lane = lax.rem(lax.broadcasted_iota(jnp.int32, (C, cols), 1), W)

    def before(value):
        return jnp.where(lane == 0, 0.0, pltpu.roll(value, 1, 1))

    def after(value):
        return jnp.where(lane == W - 1, 0.0, pltpu.roll(value, cols - 1, 1))

    def near_copy(index, X, number):
        z, y = NEAR[number]
        src_p, dst_p = {0: ((1, dl), (1, dl)), 1: ((dl, 1), (0, 1)), -1: ((1, 1), (dl + 1, 1))}[y]
        src_c, dst_c = {
            0: ((W, cols), (W, cols)),
            1: ((cols, W), (0, W)),
            -1: ((W, W), (cols + W, W)),
        }[z]
        return remote(
            X.at[pl.ds(*src_p), :, pl.ds(*src_c)],
            X.at[pl.ds(*dst_p), :, pl.ds(*dst_c)],
            near_send.at[index, number],
            near_recv.at[index, number],
            at(y, z),
        )

    def inside(z, y):
        return (f + z >= 0) & (f + z < m) & (d + y >= 0) & (d + y < n)

    def near_start(index, X):
        for number, (z, y) in enumerate(NEAR):
            @pl.when(inside(z, y))
            def _():
                near_copy(index, X, number).start()

    def near_wait(index, X):
        for number, (z, y) in enumerate(NEAR):
            @pl.when(inside(-z, -y))
            def _():
                near_copy(index, X, number).wait_recv()

    def near_end(index, X):
        for number, (z, y) in enumerate(NEAR):
            @pl.when(inside(z, y))
            def _():
                near_copy(index, X, number).wait_send()

    def conv(X, weights, plane):
        total = jnp.zeros((3 * C, cols), F32)
        for a in range(3):
            for b in range(3):
                tap = 9 * a + 3 * b
                left = weights[tap : tap + 3].reshape(3 * C, C)
                total += dot(left, X[plane + a, :, b * W : b * W + cols], (1, 0))
        return before(total[:C]) + total[C : 2 * C] + after(total[2 * C :])

    def conv_back(X, weights, plane):
        parts = []
        for c in range(3):
            total = jnp.zeros((C, cols), F32)
            for a in range(3):
                for b in range(3):
                    right = X[plane + 2 - a, :, (2 - b) * W : (2 - b) * W + cols]
                    total += dot(weights[9 * a + 3 * b + c], right, (0, 0))
            parts.append(total)
        return after(parts[0]) + parts[1] + before(parts[2])

    def grad_left(D):
        left = []
        for plane in range(dl):
            value = D[plane + 1, :, W : W + cols]
            wide = value.astype(F32)
            left.append(jnp.concatenate([after(wide).astype(BF16), value, before(wide).astype(BF16)], axis=0))
        return left

    def weight_grad(left, X, out, lines):
        for number, line in enumerate(lines):
            a, b = line // 3, line % 3
            total = dot(left[0], X[a, :, b * W : b * W + cols], (1, 1))
            for plane in range(1, dl):
                total += dot(left[plane], X[plane + a, :, b * W : b * W + cols], (1, 1))
            out[3 * number : 3 * number + 3] = total.astype(BF16).reshape(3, m, 2, hb, C)

    def sum_1(index, pb, r1):
        copy = remote(pb.at[:, :, 1 - half], r1, s1_send.at[index], s1_recv.at[index], (mate, f))
        copy.start()
        return [copy]

    def sum_2(index, copies, pb, r1, z, pr):
        copies[0].wait()

        def body(t, carry):
            z[t] = (pb[t, :, half].astype(F32) + r1[t].astype(F32)).astype(BF16)
            return carry

        lax.fori_loop(0, pb.shape[0], body, 0)
        share = pb.shape[0] // groups
        out = []
        for j in range(1, groups):
            where = at(2 * j, 0)
            copy = remote(
                z.at[pl.ds((where[0] // 2) * share, share)],
                pr.at[j - 1],
                s2_send.at[index, j - 1],
                s2_recv.at[index, j - 1],
                where,
            )
            copy.start()
            out.append(copy)
        return out

    def sum_3(index, copies, z, pr, y, zr):
        for copy in copies:
            copy.wait()
        share = y.shape[0]

        def body(t, carry):
            total = z[slot * share + t].astype(F32)
            for j in range(groups - 1):
                total += pr[j, t].astype(F32)
            y[t] = total.astype(BF16)
            return carry

        lax.fori_loop(0, share, body, 0)
        out = []
        for k in range(1, m):
            where = at(0, k)
            copy = remote(
                y.at[:, where[1]], zr.at[k - 1], s3_send.at[index, k - 1], s3_recv.at[index, k - 1], where
            )
            copy.start()
            out.append(copy)
        return out

    def sum_4(index, copies, y, zr, out):
        for copy in copies:
            copy.wait()
        share = y.shape[0]
        part = pl.ds(mul(half, hb), hb)

        def body(t, carry):
            total = y[t, f].astype(F32)
            for k in range(m - 1):
                total += zr[k, t].astype(F32)
            out[slot * share + t, part, :] = total.astype(BF16)
            return carry

        lax.fori_loop(0, share, body, 0)
        piece = out.at[pl.ds(slot * share, share), part]
        copies = []
        for j in range(1, groups):
            copy = remote(piece, piece, s4_send.at[index, j - 1], s4_recv.at[index, j - 1], at(2 * j, 0))
            copy.start()
            copies.append(copy)
        return copies

    def sum_5(index, copies, out):
        for copy in copies:
            copy.wait()
        part = pl.ds(mul(half, hb), hb)
        copy = remote(out.at[:, part], out.at[:, part], s5_send.at[index], s5_recv.at[index], (mate, f))
        copy.start()
        return [copy]

    def weight_spread(index, copies, dst):
        share = dst.shape[0] // groups
        out = []
        for k in range(1, m):
            copies[k - 1].wait()
            piece = dst.at[pl.ds(slot * share, share), band(k)]
            for j in range(1, groups):
                copy = remote(
                    piece, piece, wg_send.at[index, k - 1, j - 1], wg_recv.at[index, k - 1, j - 1], at(2 * j, 0)
                )
                copy.start()
                out.append(copy)
        return out

    def weight_pass(index, copies, dst):
        out = []
        for k in range(1, m):
            for copy in copies[(k - 1) * (groups - 1) : k * (groups - 1)]:
                copy.wait()
            piece = dst.at[:, band(k)]
            copy = remote(piece, piece, wp_send.at[index, k - 1], wp_recv.at[index, k - 1], (mate, f))
            copy.start()
            out.append(copy)
        return out

    for copy in sends:
        copy.wait()
    for plane in range(dl):
        value = dot(SW[...], U[:, plane * cols : (plane + 1) * cols], (1, 0))
        pre_l[plane] = value
        XL[plane + 1, :, W : W + cols] = silu(value).astype(BF16)
    near_start(0, XL)
    wl_copies = weight_out(1, WL)
    cot_copies = []
    for k in range(1, m):
        where = at(0, k)
        copy = remote(
            cot.at[:, :, pl.ds(mul(where[1], cols), cols)],
            XG.at[pl.ds(1, dl), own, pl.ds(W, cols)],
            swap_send.at[1, k - 1],
            swap_recv.at[1, k - 1],
            where,
        )
        copy.start()
        cot_copies.append(copy)
    wm_pass = weight_spread(0, wm_copies, WM)
    wm_pass = weight_pass(0, wm_pass, WM)
    wl_pass = weight_spread(1, wl_copies, WL)
    for copy in cot_copies:
        copy.wait()
    near_start(1, XG)
    near_wait(0, XL)
    for copy in wm_pass:
        copy.wait()
    for plane in range(dl):
        value = conv(XL, WM, plane)
        pre_m[plane] = value
        XM[plane + 1, :, W : W + cols] = silu(value).astype(BF16)
    near_start(2, XM)
    wl_pass = weight_pass(1, wl_pass, WL)
    near_wait(1, XG)
    for copy in wl_pass:
        copy.wait()

    for plane in range(dl):
        value = conv_back(XG, WL, plane) * silu_slope(pre_m[plane])
        XD[plane + 1, :, W : W + cols] = value.astype(BF16)
    near_start(3, XD)
    near_wait(2, XM)
    going = {}

    def step(number, index):
        pb, r1, z, pr, y, zr = bufs[index]
        if number == 1:
            going[index] = sum_1(index, pb, r1)
        elif number == 2:
            going[index] = sum_2(index, going[index], pb, r1, z, pr)
        elif number == 3:
            going[index] = sum_3(index, going[index], z, pr, y, zr)
        elif number == 4:
            going[index] = sum_4(index, going[index], y, zr, outs[index])
        else:
            going[index] = sum_5(index, going[index], outs[index])

    left = grad_left(XG)
    weight_grad(left, XM, bufs[0][0], range(5))
    step(1, 0)
    weight_grad(left, XM, bufs[1][0], range(5, 9))
    step(1, 1)
    left = grad_left(XD)
    weight_grad(left, XL, bufs[2][0], range(5))
    step(1, 2)
    step(2, 0)
    weight_grad(left, XL, bufs[3][0], range(5, 9))
    step(1, 3)
    step(2, 1)
    near_wait(3, XD)
    left = []
    for plane in range(dl):
        value = conv_back(XD, WM, plane) * silu_slope(pre_l[plane])
        left.append(value.astype(BF16))
    total = dot(left[0], U[:, :cols], (1, 1))
    for plane in range(1, dl):
        total += dot(left[plane], U[:, plane * cols : (plane + 1) * cols], (1, 1))
    total = total.astype(BF16)
    for pair in range(4):
        bufs[4][0][pair] = total[:, pair * 2 * CI : (pair + 1) * 2 * CI].reshape(bufs[4][0].shape[1:])
    step(1, 4)
    for number, index in ((2, 2), (2, 3), (2, 4), (3, 0), (3, 1)):
        step(number, index)

    for plane in range(dl):
        R[plane] = conv(XM, WL, plane).astype(BF16)
    out_spot = pl.ds(mul(f, cols), cols)
    out_copies = []
    for k in range(1, m):
        where = at(0, k)
        copy = remote(
            R.at[:, pl.ds(mul(where[1], oc), oc)],
            res.at[:, :, out_spot],
            swap_send.at[2, k - 1],
            swap_recv.at[2, k - 1],
            where,
        )
        copy.start()
        out_copies.append(copy)
    res[:, :, out_spot] = R[:, own]

    for number, index in (
        (3, 2), (4, 0), (3, 3), (4, 1), (3, 4), (5, 0), (4, 2), (5, 1), (4, 3), (4, 4), (5, 2), (5, 3), (5, 4)
    ):
        step(number, index)
    for copy in out_copies + [copy for copies in going.values() for copy in copies]:
        copy.wait()
    for index, X in enumerate((XL, XG, XM, XD)):
        near_end(index, X)


def per_device(n, m, upper_level, stride_weight, middle_weight, last_weight, cotangent):
    oc, dl, H, W = cotangent.shape
    hl = H // m
    C, CI = oc * m, upper_level.shape[0]
    T = middle_weight.shape[0]
    hb = oc // 2
    up = upper_level.transpose(1, 2, 0, 3).reshape(4 * dl * hl, CI, 2 * W)
    cot = cotangent.transpose(1, 0, 2, 3).reshape(dl, oc, H * W)
    wide = pltpu.VMEM((dl + 2, C, (hl + 2) * W), BF16)

    groups = n // 2
    TP = -(-T // groups) * groups
    sizes = [-(-count // groups) * groups for count in CHUNKS]
    lanes = [C] * 4 + [2 * CI]

    def sums(count, lanes):
        share = count // groups
        return [
            pltpu.VMEM((count, m, 2, hb, lanes), BF16),
            pltpu.VMEM((count, m, hb, lanes), BF16),
            pltpu.VMEM((count, m, hb, lanes), BF16),
            pltpu.VMEM((groups - 1, share, m, hb, lanes), BF16),
            pltpu.VMEM((share, m, hb, lanes), BF16),
            pltpu.VMEM((m - 1, share, hb, lanes), BF16),
        ]

    def sems(*shape):
        return [pltpu.SemaphoreType.DMA(shape)] * 2

    res, *grads = pl.pallas_call(
        functools.partial(kernel, n, m, dl, hl, W),
        out_shape=(
            jax.ShapeDtypeStruct((dl, oc, H * W), BF16),
            *(jax.ShapeDtypeStruct((size, oc, wide_), BF16) for size, wide_ in zip(sizes, lanes)),
        ),
        in_specs=[pl.BlockSpec(memory_space=pltpu.VMEM)] * 5,
        out_specs=[pl.BlockSpec(memory_space=pltpu.VMEM)] * 6,
        scratch_shapes=[
            pltpu.VMEM((C, 8 * CI), BF16),
            pltpu.VMEM((TP, C, C), BF16),
            pltpu.VMEM((TP, C, C), BF16),
            wide, wide, wide, wide,
            pltpu.VMEM((8 * CI, dl * hl * W), BF16),
            pltpu.VMEM((dl, C, hl * W), F32),
            pltpu.VMEM((dl, C, hl * W), F32),
            pltpu.VMEM((dl, C, hl * W), BF16),
            *(buf for size, wide_ in zip(sizes, lanes) for buf in sums(size, wide_)),
            *sems(4, 8),
            *sems(3, m - 1),
            *sems(2, m - 1),
            *sems(2, m - 1, groups - 1),
            *sems(2, m - 1),
            *sems(5),
            *sems(5, groups - 1),
            *sems(5, m - 1),
            *sems(5, groups - 1),
            *sems(5),
        ],
        compiler_params=pltpu.CompilerParams(
            collective_id=0, has_side_effects=True, vmem_limit_bytes=52 * 1024 * 1024
        ),
    )(up, stride_weight, middle_weight, last_weight, cot)
    result = res.reshape(dl, oc, H, W).transpose(1, 0, 2, 3)
    gs, gm, gl = pl.pallas_call(
        widen,
        out_shape=(
            jax.ShapeDtypeStruct((8, oc, CI), F32),
            jax.ShapeDtypeStruct((T, oc, C), F32),
            jax.ShapeDtypeStruct((T, oc, C), F32),
        ),
    )(*grads)
    return (result, gs, gm, gl)


def widen(last_0, last_1, middle_0, middle_1, stride, gs, gm, gl):
    for source, target, start, count in (
        (last_0, gl, 0, CHUNKS[0]),
        (last_1, gl, CHUNKS[0], CHUNKS[1]),
        (middle_0, gm, 0, CHUNKS[2]),
        (middle_1, gm, CHUNKS[2], CHUNKS[3]),
    ):
        target[start : start + count] = source[:count].astype(F32)
    CI = gs.shape[2]
    for tap in range(8):
        gs[tap] = stride[tap // 2].astype(F32)[:, (tap % 2) * CI : (tap % 2 + 1) * CI]


def solution(mesh):
    weights = P(None, "filt", None)
    cells = P("filt", "depth", None, None)
    return jax.shard_map(
        functools.partial(per_device, mesh.shape["depth"], mesh.shape["filt"]),
        mesh=mesh,
        in_specs=(P(None, "depth", "filt", None), weights, weights, weights, cells),
        out_specs=(cells, weights, weights, weights),
        check_vma=False,
    )
```

```python
import functools

import jax
import jax.numpy as jnp
from jax import lax
from jax.experimental import pallas as pl
from jax.experimental.pallas import tpu as pltpu
from jax.sharding import PartitionSpec as P

F32 = jnp.float32
BF16 = jnp.bfloat16
MESH = pl.DeviceIdType.MESH
CHUNKS = (15, 12, 15, 12)
NEAR = [(z, y) for z in (-1, 0, 1) for y in (-1, 0, 1) if (z, y) != (0, 0)]


def dot(left, right, dims):
    return lax.dot_general(left, right, ((dims[:1], dims[1:]), ((), ())), preferred_element_type=F32)


def silu_slope(value):
    sigma = 1.0 / (1.0 + jnp.exp(-value))
    return sigma * (1.0 + value * (1.0 - sigma))


def silu(value):
    return value / (1.0 + jnp.exp(-value))


def kernel(
    n, m, dl, hl, W,
    up, sw, wm, wl, cot,
    *refs,
):
    res, *outs = refs[:6]
    SW, WM, WL, XL, XM, XG, XD, U, pre_l, pre_m, R = refs[6:17]
    bufs = [refs[17 + 6 * i : 23 + 6 * i] for i in range(4)]
    pb_s, zr_s, dr_s = refs[41:44]
    (
    near_send, near_recv, swap_send, swap_recv,
    wz_send, wz_recv, wg_send, wg_recv, wp_send, wp_recv,
    s1_send, s1_recv, s2_send, s2_recv, s3_send, s3_recv, s4_send, s4_recv,
    ) = refs[44:]
    d, f = lax.axis_index("depth"), lax.axis_index("filt")
    oc, C = cot.shape[1], WM.shape[1]
    CI = up.shape[1]
    hb = oc // 2
    T = wm.shape[0]
    groups = n // 2
    half, slot = lax.rem(d, 2), d // 2
    mate = d + 1 - 2 * half
    cols = hl * W

    for X in (XL, XM, XG, XD):
        X[...] = jnp.zeros_like(X)
    for X, used in ((WM, T), (WL, T), *((bufs[i][0], CHUNKS[i]) for i in range(4))):
        if X.shape[0] > used:
            X[used:] = jnp.zeros((X.shape[0] - used,) + X.shape[1:], X.dtype)
    own = pl.ds(pl.multiple_of(f * oc, oc), oc)
    WM[:T, own, :] = wm[...]
    WL[:T, own, :] = wl[...]
    for tap in range(8):
        SW[own, tap * CI : (tap + 1) * CI] = sw[tap]

    def at(steps_d, steps_f):
        return (lax.rem(d + steps_d + n, n), lax.rem(f + steps_f + m, m))

    barrier = pltpu.get_barrier_semaphore()
    greet = [(0, k) for k in range(1, m)] + [(y, z) for z, y in NEAR if y != 0]
    greet += [(j, 0) for j in range(2, n - 1)]
    for step in greet:
        pl.semaphore_signal(barrier, inc=1, device_id=at(*step), device_id_type=MESH)
    pl.semaphore_wait(barrier, len(greet))

    def remote(src, dst, send, recv, where):
        return pltpu.make_async_remote_copy(
            src_ref=src, dst_ref=dst, send_sem=send, recv_sem=recv, device_id=where, device_id_type=MESH
        )

    def mul(value, by):
        return pl.multiple_of(value * by, by)

    sends = []
    for k in range(1, m):
        where = at(0, k)
        copy = remote(SW.at[own], SW.at[own], swap_send.at[0, k - 1], swap_recv.at[0, k - 1], where)
        copy.start()
        sends.append(copy)

    def band(k):
        return pl.ds(pl.multiple_of(lax.rem(f - k + m, m) * oc + half * hb, hb), hb)

    def weight_out(index, dst):
        copies = []
        share = dst.shape[0] // groups
        piece = dst.at[pl.ds(slot * share, share), band(0)]
        for k in range(1, m):
            copy = remote(piece, piece, wz_send.at[index, k - 1], wz_recv.at[index, k - 1], at(0, k))
            copy.start()
            copies.append(copy)
        return copies

    wm_copies = weight_out(0, WM)
    wl_copies = weight_out(1, WL)
    cot_copies = []
    for k in range(1, m):
        where = at(0, k)
        copy = remote(
            cot.at[:, :, pl.ds(mul(where[1], cols), cols)],
            XG.at[pl.ds(1, dl), own, pl.ds(W, cols)],
            swap_send.at[1, k - 1],
            swap_recv.at[1, k - 1],
            where,
        )
        copy.start()
        cot_copies.append(copy)
    XG[pl.ds(1, dl), own, pl.ds(W, cols)] = cot[:, :, pl.ds(mul(f, cols), cols)]

    line = lax.broadcasted_iota(jnp.int32, (2 * W, 2 * W), 0)
    column = lax.broadcasted_iota(jnp.int32, (2 * W, 2 * W), 1)
    wanted = jnp.where(column < W, 2 * column, 2 * (column - W) + 1)
    pick = jnp.where(line == wanted, 1.0, 0.0).astype(BF16)
    for plane in range(2 * dl):
        for row in range(2 * hl):
            both = dot(up[plane * 2 * hl + row], pick, (1, 0)).astype(BF16)
            tap = 4 * (plane % 2) + 2 * (row % 2)
            place = ((plane // 2) * hl + row // 2) * W
            U[tap * CI : (tap + 1) * CI, place : place + W] = both[:, :W]
            U[(tap + 1) * CI : (tap + 2) * CI, place : place + W] = both[:, W:]

    lane = lax.rem(lax.broadcasted_iota(jnp.int32, (C, cols), 1), W)

    def before(value):
        return jnp.where(lane == 0, 0.0, pltpu.roll(value, 1, 1))

    def after(value):
        return jnp.where(lane == W - 1, 0.0, pltpu.roll(value, cols - 1, 1))

    def near_copy(index, X, number):
        z, y = NEAR[number]
        src_p, dst_p = {0: ((1, dl), (1, dl)), 1: ((dl, 1), (0, 1)), -1: ((1, 1), (dl + 1, 1))}[y]
        src_c, dst_c = {
            0: ((W, cols), (W, cols)),
            1: ((cols, W), (0, W)),
            -1: ((W, W), (cols + W, W)),
        }[z]
        return remote(
            X.at[pl.ds(*src_p), :, pl.ds(*src_c)],
            X.at[pl.ds(*dst_p), :, pl.ds(*dst_c)],
            near_send.at[index, number],
            near_recv.at[index, number],
            at(y, z),
        )

    def inside(z, y):
        return (f + z >= 0) & (f + z < m) & (d + y >= 0) & (d + y < n)

    def near_start(index, X):
        for number, (z, y) in enumerate(NEAR):
            @pl.when(inside(z, y))
            def _():
                near_copy(index, X, number).start()

    def near_wait(index, X):
        for number, (z, y) in enumerate(NEAR):
            @pl.when(inside(-z, -y))
            def _():
                near_copy(index, X, number).wait_recv()

    def near_end(index, X):
        for number, (z, y) in enumerate(NEAR):
            @pl.when(inside(z, y))
            def _():
                near_copy(index, X, number).wait_send()

    def conv(X, weights, plane):
        total = jnp.zeros((3 * C, cols), F32)
        for a in range(3):
            for b in range(3):
                tap = 9 * a + 3 * b
                left = weights[tap : tap + 3].reshape(3 * C, C)
                total += dot(left, X[plane + a, :, b * W : b * W + cols], (1, 0))
        return before(total[:C]) + total[C : 2 * C] + after(total[2 * C :])

    def conv_back(X, weights, plane):
        parts = []
        for c in range(3):
            total = jnp.zeros((C, cols), F32)
            for a in range(3):
                for b in range(3):
                    right = X[plane + 2 - a, :, (2 - b) * W : (2 - b) * W + cols]
                    total += dot(weights[9 * a + 3 * b + c], right, (0, 0))
            parts.append(total)
        return after(parts[0]) + parts[1] + before(parts[2])

    def grad_left(D):
        left = []
        for plane in range(dl):
            value = D[plane + 1, :, W : W + cols]
            wide = value.astype(F32)
            left.append(jnp.concatenate([after(wide).astype(BF16), value, before(wide).astype(BF16)], axis=0))
        return left

    def weight_grad(left, X, out, lines):
        for number, line in enumerate(lines):
            a, b = line // 3, line % 3
            total = dot(left[0], X[a, :, b * W : b * W + cols], (1, 1))
            for plane in range(1, dl):
                total += dot(left[plane], X[plane + a, :, b * W : b * W + cols], (1, 1))
            out[3 * number : 3 * number + 3] = total.astype(BF16).reshape(3, m, 2, hb, C)

    def sum_1(index, pb, r1):
        copy = remote(pb.at[:, :, 1 - half], r1, s1_send.at[index], s1_recv.at[index], (mate, f))
        copy.start()
        return [copy]

    def sum_2(index, copies, pb, r1, z, pr):
        copies[0].wait()

        for t in range(pb.shape[0]):
            z[t] = (pb[t, :, half].astype(F32) + r1[t].astype(F32)).astype(BF16)
        share = pb.shape[0] // groups
        out = []
        for j in range(1, groups):
            where = at(2 * j, 0)
            copy = remote(
                z.at[pl.ds((where[0] // 2) * share, share)],
                pr.at[j - 1],
                s2_send.at[index, j - 1],
                s2_recv.at[index, j - 1],
                where,
            )
            copy.start()
            out.append(copy)
        return out

    def sum_3(index, copies, z, pr, y, zr):
        for copy in copies:
            copy.wait()
        share = y.shape[0]

        for t in range(share):
            total = z[slot * share + t].astype(F32)
            for j in range(groups - 1):
                total += pr[j, t].astype(F32)
            y[t] = total.astype(BF16)
        out = []
        for k in range(1, m):
            where = at(0, k)
            copy = remote(
                y.at[:, where[1]], zr.at[k - 1], s3_send.at[index, k - 1], s3_recv.at[index, k - 1], where
            )
            copy.start()
            out.append(copy)
        return out

    def sum_4(index, copies, y, zr, out):
        for copy in copies:
            copy.wait()
        share = y.shape[0]
        part = pl.ds(mul(half, hb), hb)

        for t in range(share):
            total = y[t, f].astype(F32)
            for k in range(m - 1):
                total += zr[k, t].astype(F32)
            out[slot * share + t, part, :] = total.astype(BF16)
        piece = out.at[pl.ds(slot * share, share), part]
        copies = []
        for j in range(1, n):
            copy = remote(piece, piece, s4_send.at[index, j - 1], s4_recv.at[index, j - 1], at(j, 0))
            copy.start()
            copies.append(copy)
        return copies

    def stride_1():
        copies = []
        for k in range(1, m):
            where = at(0, k)
            copy = remote(pb_s.at[where[1]], zr_s.at[k - 1], s3_send.at[4, k - 1], s3_recv.at[4, k - 1], where)
            copy.start()
            copies.append(copy)
        return copies

    def stride_2(copies):
        for copy in copies:
            copy.wait()
        total = pb_s[f].astype(F32)
        for k in range(m - 1):
            total += zr_s[k].astype(F32)
        dr_s[d] = total.astype(BF16)
        copies = []
        for j in range(1, n):
            copy = remote(dr_s.at[d], dr_s.at[d], s4_send.at[4, j - 1], s4_recv.at[4, j - 1], at(j, 0))
            copy.start()
            copies.append(copy)
        return copies

    def stride_3(copies):
        for copy in copies:
            copy.wait()
        total = dr_s[0].astype(F32)
        for j in range(1, n):
            total += dr_s[j].astype(F32)
        outs[4][...] = total

    def weight_spread(index, copies, dst):
        share = dst.shape[0] // groups
        out = []
        for k in range(1, m):
            copies[k - 1].wait()
            piece = dst.at[pl.ds(slot * share, share), band(k)]
            for j in range(1, groups):
                copy = remote(
                    piece, piece, wg_send.at[index, k - 1, j - 1], wg_recv.at[index, k - 1, j - 1], at(2 * j, 0)
                )
                copy.start()
                out.append(copy)
        return out

    def weight_pass(index, copies, dst):
        out = []
        for k in range(1, m):
            for copy in copies[(k - 1) * (groups - 1) : k * (groups - 1)]:
                copy.wait()
            piece = dst.at[:, band(k)]
            copy = remote(piece, piece, wp_send.at[index, k - 1], wp_recv.at[index, k - 1], (mate, f))
            copy.start()
            out.append(copy)
        return out

    for copy in sends:
        copy.wait()
    for plane in range(dl):
        value = dot(SW[...], U[:, plane * cols : (plane + 1) * cols], (1, 0))
        pre_l[plane] = value
        XL[plane + 1, :, W : W + cols] = silu(value).astype(BF16)
    near_start(0, XL)
    wm_pass = weight_spread(0, wm_copies, WM)
    wm_pass = weight_pass(0, wm_pass, WM)
    wl_pass = weight_spread(1, wl_copies, WL)
    for copy in cot_copies:
        copy.wait()
    near_start(1, XG)
    near_wait(0, XL)
    for copy in wm_pass:
        copy.wait()
    for plane in range(dl):
        value = conv(XL, WM, plane)
        pre_m[plane] = value
        XM[plane + 1, :, W : W + cols] = silu(value).astype(BF16)
    near_start(2, XM)
    wl_pass = weight_pass(1, wl_pass, WL)
    near_wait(1, XG)
    for copy in wl_pass:
        copy.wait()

    for plane in range(dl):
        value = conv_back(XG, WL, plane) * silu_slope(pre_m[plane])
        XD[plane + 1, :, W : W + cols] = value.astype(BF16)
    near_start(3, XD)
    near_wait(2, XM)
    going = {}

    def step(number, index):
        pb, r1, z, pr, y, zr = bufs[index]
        if number == 1:
            going[index] = sum_1(index, pb, r1)
        elif number == 2:
            going[index] = sum_2(index, going[index], pb, r1, z, pr)
        elif number == 3:
            going[index] = sum_3(index, going[index], z, pr, y, zr)
        else:
            going[index] = sum_4(index, going[index], y, zr, outs[index])

    left = grad_left(XG)
    weight_grad(left, XM, bufs[0][0], range(5))
    step(1, 0)
    weight_grad(left, XM, bufs[1][0], range(5, 9))
    step(1, 1)
    left = grad_left(XD)
    weight_grad(left, XL, bufs[2][0], range(5))
    step(1, 2)
    step(2, 0)
    weight_grad(left, XL, bufs[3][0], range(5, 9))
    step(1, 3)
    step(2, 1)
    near_wait(3, XD)
    left = []
    for plane in range(dl):
        value = conv_back(XD, WM, plane) * silu_slope(pre_l[plane])
        left.append(value.astype(BF16))
    total = dot(left[0], U[:, :cols], (1, 1))
    for plane in range(1, dl):
        total += dot(left[plane], U[:, plane * cols : (plane + 1) * cols], (1, 1))
    pb_s[...] = total.astype(BF16).reshape(pb_s.shape)
    stride = stride_1()
    for number, index in ((2, 2), (2, 3), (3, 0), (3, 1)):
        step(number, index)
    stride = stride_2(stride)

    for plane in range(dl):
        R[plane] = conv(XM, WL, plane).astype(BF16)
    out_spot = pl.ds(mul(f, cols), cols)
    out_copies = []
    for k in range(1, m):
        where = at(0, k)
        copy = remote(
            R.at[:, pl.ds(mul(where[1], oc), oc)],
            res.at[:, :, out_spot],
            swap_send.at[2, k - 1],
            swap_recv.at[2, k - 1],
            where,
        )
        copy.start()
        out_copies.append(copy)
    res[:, :, out_spot] = R[:, own]

    for number, index in ((3, 2), (3, 3), (4, 0), (4, 1), (4, 2), (4, 3)):
        step(number, index)
    stride_3(stride)
    for copy in out_copies + [copy for copies in going.values() for copy in copies]:
        copy.wait()
    for index, X in enumerate((XL, XG, XM, XD)):
        near_end(index, X)


def per_device(n, m, upper_level, stride_weight, middle_weight, last_weight, cotangent):
    oc, dl, H, W = cotangent.shape
    hl = H // m
    C, CI = oc * m, upper_level.shape[0]
    T = middle_weight.shape[0]
    hb = oc // 2
    up = upper_level.transpose(1, 2, 0, 3).reshape(4 * dl * hl, CI, 2 * W)
    cot = cotangent.transpose(1, 0, 2, 3).reshape(dl, oc, H * W)
    wide = pltpu.VMEM((dl + 2, C, (hl + 2) * W), BF16)

    groups = n // 2
    TP = -(-T // groups) * groups
    sizes = [-(-count // groups) * groups for count in CHUNKS]

    def sums(count, lanes):
        share = count // groups
        return [
            pltpu.VMEM((count, m, 2, hb, lanes), BF16),
            pltpu.VMEM((count, m, hb, lanes), BF16),
            pltpu.VMEM((count, m, hb, lanes), BF16),
            pltpu.VMEM((groups - 1, share, m, hb, lanes), BF16),
            pltpu.VMEM((share, m, hb, lanes), BF16),
            pltpu.VMEM((m - 1, share, hb, lanes), BF16),
        ]

    def sems(*shape):
        return [pltpu.SemaphoreType.DMA(shape)] * 2

    res, *grads = pl.pallas_call(
        functools.partial(kernel, n, m, dl, hl, W),
        out_shape=(
            jax.ShapeDtypeStruct((dl, oc, H * W), BF16),
            *(jax.ShapeDtypeStruct((size, oc, C), BF16) for size in sizes),
            jax.ShapeDtypeStruct((oc, 8 * CI), F32),
        ),
        in_specs=[pl.BlockSpec(memory_space=pltpu.VMEM)] * 5,
        out_specs=[pl.BlockSpec(memory_space=pltpu.VMEM)] * 6,
        scratch_shapes=[
            pltpu.VMEM((C, 8 * CI), BF16),
            pltpu.VMEM((TP, C, C), BF16),
            pltpu.VMEM((TP, C, C), BF16),
            wide, wide, wide, wide,
            pltpu.VMEM((8 * CI, dl * hl * W), BF16),
            pltpu.VMEM((dl, C, hl * W), F32),
            pltpu.VMEM((dl, C, hl * W), F32),
            pltpu.VMEM((dl, C, hl * W), BF16),
            *(buf for size in sizes for buf in sums(size, C)),
            pltpu.VMEM((m, oc, 8 * CI), BF16),
            pltpu.VMEM((m - 1, oc, 8 * CI), BF16),
            pltpu.VMEM((n, oc, 8 * CI), BF16),
            *sems(4, 8),
            *sems(3, m - 1),
            *sems(2, m - 1),
            *sems(2, m - 1, groups - 1),
            *sems(2, m - 1),
            *sems(4),
            *sems(4, groups - 1),
            *sems(5, m - 1),
            *sems(5, n - 1),
        ],
        compiler_params=pltpu.CompilerParams(
            collective_id=0, has_side_effects=True, vmem_limit_bytes=52 * 1024 * 1024
        ),
    )(up, stride_weight, middle_weight, last_weight, cot)
    result = res.reshape(dl, oc, H, W).transpose(1, 0, 2, 3)
    gs, gm, gl = pl.pallas_call(
        widen,
        out_shape=(
            jax.ShapeDtypeStruct((8, oc, CI), F32),
            jax.ShapeDtypeStruct((T, oc, C), F32),
            jax.ShapeDtypeStruct((T, oc, C), F32),
        ),
    )(*grads)
    return (result, gs, gm, gl)


def widen(last_0, last_1, middle_0, middle_1, stride, gs, gm, gl):
    for source, target, start, count in (
        (last_0, gl, 0, CHUNKS[0]),
        (last_1, gl, CHUNKS[0], CHUNKS[1]),
        (middle_0, gm, 0, CHUNKS[2]),
        (middle_1, gm, CHUNKS[2], CHUNKS[3]),
    ):
        target[start : start + count] = source[:count].astype(F32)
    CI = gs.shape[2]
    for tap in range(8):
        gs[tap] = stride[:, tap * CI : (tap + 1) * CI]


def solution(mesh):
    weights = P(None, "filt", None)
    cells = P("filt", "depth", None, None)
    return jax.shard_map(
        functools.partial(per_device, mesh.shape["depth"], mesh.shape["filt"]),
        mesh=mesh,
        in_specs=(P(None, "depth", "filt", None), weights, weights, weights, cells),
        out_specs=(cells, weights, weights, weights),
        check_vma=False,
    )
```
